32 devices in a mesh: grp: 2 (over x), wide: 8 (over z, y), narrow: 2 (over core).
Axes of the slice: x: 2, y: 2, z: 4, core: 2. Of those that a mesh axis runs over, the one named last changes fastest.
Arguments:
- video: bfloat16 [16, 64, 32, 128], P(('grp', 'wide')), parts along dimension 0, may hold values from -6 to 6
- spatial_weight: bfloat16 [144, 9, 64], replicated, may hold values from -0.25 to 0.25
- spatial_bias: float32 [144], replicated, may hold values from -4 to 4
- temporal_weight: bfloat16 [64, 9, 144], replicated, may hold values from -0.15625 to 0.15625
- temporal_bias: float32 [64], replicated, may hold values from -4 to 4
- out_cotangent: bfloat16 [8, 64, 32, 128], P('grp', None, ('wide', 'narrow')), parts along dimension 0, may hold values from -6 to 6
Outputs:
- output: bfloat16 [8, 64, 32, 128], P('grp', None, ('wide', 'narrow')), parts along dimension 0
- grad_video: bfloat16 [16, 64, 32, 128], P(('grp', 'wide'), None, 'narrow'), parts along dimension 0
- grad_spatial: float32 [288, 9, 64], P(('grp', 'narrow')), parts along dimension 0
- grad_temporal: float32 [128, 9, 144], P('grp'), parts along dimension 0
The draws below stay inside these ranges and needn't reach their ends.
There are 2 independent parts, one for each index of `grp`. The reference program is written for one: setup_inputs(seed, part) draws one part's arguments, and reference() takes and returns one part's arrays. A program takes and returns all parts, laid end to end along the dimension named above; an argument that names none is the same for every part. Nothing has to cross between parts.
All inputs are finite; a program needn't handle non-finite values.
Results may differ from the reference program's by a relative error of at most 0.0058.
Values may be sent and summed in bfloat16 or wider, within the bound.
A program may use at most 128 MiB of HBM per device.

```python
import math
import jax
import jax.numpy as jnp

CIN = 64
CMID = 144
COUT = 64
TAPS = 9
COLS = 128
FRAMES = 8
OUT_FRAMES = 4
ROWS = 32


def shard_levels(stream_key, shape, split, low, high):
    gain, own = 1.0, jax.random.fold_in(stream_key, 6)
    for axis_at, shards_of in split:
        draws = jnp.exp(jax.random.uniform(jax.random.fold_in(own, axis_at), (shards_of,), jnp.float32, low / len(split), high / len(split)))
        gain = gain * jnp.repeat(draws, shape[axis_at] // shards_of).reshape([-1 if axis == axis_at else 1 for axis in range(len(shape))])
    return gain


def gaussian(key, extent, scale, limit, pieces=(), held_as=jnp.bfloat16):
    values = scale * jax.random.normal(key, extent, jnp.float32)
    if pieces:
        values = values * shard_levels(key, extent, pieces, -0.22, 0.18)
    return jnp.clip(values, -limit, limit).astype(held_as)


def setup_inputs(seed: int = 0, part: int = 0) -> dict:
    key_of = jax.random.split(jax.random.key(seed), 7)
    own_keys = jax.random.split(jax.random.fold_in(key_of[6], part), 7)
    return {
        "video": gaussian(own_keys[0], (FRAMES, CIN, ROWS, COLS), 1.0, 6.0, ((0, 8),)),
        "spatial_weight": gaussian(key_of[1], (CMID, 9, CIN), (9 * CIN) ** -0.5, 0.25),
        "spatial_bias": gaussian(key_of[2], (CMID,), 1.0, 4.0, (), jnp.float32),
        "temporal_weight": gaussian(key_of[3], (COUT, TAPS, CMID), (TAPS * CMID) ** -0.5, 0.15625),
        "temporal_bias": gaussian(key_of[4], (COUT,), 1.0, 4.0, (), jnp.float32),
        "out_cotangent": gaussian(own_keys[5], (OUT_FRAMES, COUT, ROWS, COLS), 1.0, 6.0, ((2, 16),)),
    }


def silu_slope(preact):
    logistic = jax.nn.sigmoid(preact)
    return logistic * (1.0 + preact * (1.0 - logistic))

def reference(video, spatial_weight, spatial_bias, temporal_weight, temporal_bias, out_cotangent):
    pixel_count = ROWS * COLS
    half_taps = TAPS // 2
    grid_weight = spatial_weight.astype(jnp.float32).reshape(CMID, 3, 3, CIN)
    padded_video = jnp.pad(video.astype(jnp.float32), ((0, 0), (0, 0), (1, 1), (1, 1)))
    preact = jnp.zeros((FRAMES, CMID, ROWS, COLS), jnp.float32) + spatial_bias[None, :, None, None]
    for row_shift in range(3):
        for col_shift in range(3):
            window = padded_video[:, :, row_shift:row_shift + ROWS, col_shift:col_shift + COLS]
            preact = preact + jnp.einsum('oc,fcyx->foyx', grid_weight[:, row_shift, col_shift], window)
    activation = jax.nn.silu(preact).astype(jnp.bfloat16)
    flat_act = activation.astype(jnp.float32).reshape(FRAMES, CMID, pixel_count)
    padded_act = jnp.pad(flat_act, ((half_taps, half_taps), (0, 0), (0, 0)))
    tap_weight = temporal_weight.astype(jnp.float32)
    cotangent = out_cotangent.astype(jnp.float32).reshape(OUT_FRAMES, COUT, pixel_count)
    combined = jnp.zeros((OUT_FRAMES, COUT, pixel_count), jnp.float32) + temporal_bias[None, :, None]
    grad_taps = []
    padded_grad = jnp.zeros((FRAMES + 2 * half_taps, CMID, pixel_count), jnp.float32)
    for offset in range(TAPS):
        tap_slab = padded_act[offset:offset + 2 * OUT_FRAMES:2]
        combined = combined + jnp.einsum('oc,tcp->top', tap_weight[:, offset], tap_slab)
        grad_taps.append(jnp.einsum('top,tcp->oc', cotangent, tap_slab))
        contribution = jnp.einsum('oc,top->tcp', tap_weight[:, offset], cotangent)
        padded_grad = padded_grad.at[offset:offset + 2 * OUT_FRAMES:2].add(contribution)
    output = combined.astype(jnp.bfloat16).reshape(OUT_FRAMES, COUT, ROWS, COLS)
    grad_temporal = jnp.stack(grad_taps, axis=1) / math.sqrt(OUT_FRAMES * pixel_count)
    grad_act = padded_grad[half_taps:half_taps + FRAMES].astype(jnp.bfloat16).reshape(FRAMES, CMID, ROWS, COLS)
    grad_pre = (grad_act.astype(jnp.float32) * silu_slope(preact)).astype(jnp.bfloat16)
    grad_wide = grad_pre.astype(jnp.float32)
    spatial_terms = []
    for row_shift in range(3):
        for col_shift in range(3):
            window = padded_video[:, :, row_shift:row_shift + ROWS, col_shift:col_shift + COLS]
            spatial_terms.append(jnp.einsum('foyx,fcyx->oc', grad_wide, window))
    grad_spatial = jnp.stack(spatial_terms, axis=1) / math.sqrt(FRAMES * pixel_count)
    padded_pre = jnp.pad(grad_wide, ((0, 0), (0, 0), (1, 1), (1, 1)))
    grad_video = jnp.zeros((FRAMES, CIN, ROWS, COLS), jnp.float32)
    for row_shift in range(3):
        for col_shift in range(3):
            window = padded_pre[:, :, 2 - row_shift:2 - row_shift + ROWS, 2 - col_shift:2 - col_shift + COLS]
            grad_video = grad_video + jnp.einsum('oc,foyx->fcyx', grid_weight[:, row_shift, col_shift], window)
    return (output, grad_video.astype(jnp.bfloat16), grad_spatial, grad_temporal)
```

```python
import functools
import math

import jax
import jax.numpy as jnp
from jax import lax
from jax.experimental import pallas as pl
from jax.experimental.pallas import tpu as pltpu
from jax.sharding import PartitionSpec as P

MESH = pl.DeviceIdType.MESH
BF16 = jnp.bfloat16
F32 = jnp.float32
VMEM_BYTES = 50 * 1024 * 1024


def greet_all(wide_count):
    me = lax.axis_index("wide") * 2 + lax.axis_index("narrow")
    total = 2 * wide_count
    barrier = pltpu.get_barrier_semaphore()

    def greet(k, carry):
        other = lax.rem(me + k, total)
        pl.semaphore_signal(
            barrier, inc=1, device_id={"wide": other // 2, "narrow": lax.rem(other, 2)}, device_id_type=MESH
        )
        return carry

    lax.fori_loop(1, total, greet, 0)
    pl.semaphore_wait(barrier, total - 1)


def remote(src, dst, send_sem, recv_sem, wide, narrow):
    return pltpu.make_async_remote_copy(
        src_ref=src,
        dst_ref=dst,
        send_sem=send_sem,
        recv_sem=recv_sem,
        device_id={"wide": wide, "narrow": narrow},
        device_id_type=MESH,
    )


def gather_kernel(W, tr, v_ref, g_ref, slab_ref, halo_ref, ssem, rsem, fssem, frsem, hs, hr, lsem):
    w = lax.axis_index("wide")
    n = lax.axis_index("narrow")
    half = tr + 2
    greet_all(W)
    place = 2 * n

    me = w * 2 + n
    nxt = lax.rem(me + 1, 2 * W)
    prv = lax.rem(me + 2 * W - 1, 2 * W)
    down = remote(g_ref.at[tr - 1], halo_ref.at[0], hs.at[0], hr.at[0], nxt // 2, lax.rem(nxt, 2))
    up = remote(g_ref.at[0], halo_ref.at[1], hs.at[1], hr.at[1], prv // 2, lax.rem(prv, 2))

    def outgoing(dst):
        return remote(
            v_ref.at[pl.ds(2 * tr * dst + half * n, half)],
            slab_ref.at[w, pl.ds(place, half)],
            ssem.at[dst],
            rsem.at[w],
            dst,
            n,
        )

    def forward(src):
        return remote(
            slab_ref.at[src, pl.ds(tr * (1 - n) + 2 * n, 2)],
            slab_ref.at[src, pl.ds(half * n, 2)],
            fssem.at[src],
            frsem.at[src],
            w,
            1 - n,
        )

    def start(k, carry):
        outgoing(lax.rem(w + k, W)).start()
        return carry

    lax.fori_loop(1, W, start, 0)
    own = pltpu.make_async_copy(
        v_ref.at[pl.ds(2 * tr * w + tr * n, tr + 4)], slab_ref.at[w], lsem
    )
    own.start()
    down.start()
    up.start()

    def relay(k, carry):
        src = lax.rem(w + W - k, W)
        remote(
            v_ref.at[pl.ds(0, half)], slab_ref.at[src, pl.ds(place, half)], ssem.at[src], rsem.at[src], src, n
        ).wait_recv()
        forward(src).start()
        return carry

    lax.fori_loop(1, W, relay, 0)
    own.wait()

    def finish(k, carry):
        src = lax.rem(w + W - k, W)
        fwd = remote(
            slab_ref.at[src, pl.ds(0, 2)],
            slab_ref.at[src, pl.ds(half * (1 - n), 2)],
            fssem.at[src],
            frsem.at[src],
            w,
            1 - n,
        )
        fwd.wait_recv()
        forward(src).wait_send()
        outgoing(src).wait_send()
        return carry

    lax.fori_loop(1, W, finish, 0)
    down.wait()
    up.wait()


def nt(a, b):
    return lax.dot_general(a, b, (((1,), (1,)), ((), ())), preferred_element_type=F32)


def compute_kernel(
    W, tr, F, T, taps, pscale, tscale,
    slab_ref, g_ref, halo_ref, ws_ref, sb_ref, wv_ref, wt_ref, tb_ref, we_ref, wo_ref,
    out_ref, gv_ref, gs_ref, gt_ref,
    stack, gpad, apad, gsum, tsum,
):
    cin = slab_ref.shape[2]
    cols = slab_ref.shape[3]
    cmid = ws_ref.shape[0]
    cout = wt_ref.shape[0]
    half = taps // 2
    gp_rows = tr + 2
    px = tr * cols
    lead = half // 2
    me = lax.axis_index("wide") * 2 + lax.axis_index("narrow")

    gpad[0 : lead * cout, :] = jnp.zeros((lead * cout, gp_rows * cols), BF16)
    gpad[(lead + T) * cout :, :] = jnp.zeros((lead * cout, gp_rows * cols), BF16)
    apad[0 : half * cmid, :] = jnp.zeros((half * cmid, px), BF16)
    apad[(half + F) * cmid :, :] = jnp.zeros((half * cmid, px), BF16)
    body = slice(lead * cout, (lead + T) * cout)
    above = halo_ref[0].reshape(T * cout, cols)
    gpad[body, 0:cols] = jnp.where(me == 0, jnp.zeros_like(above), above)
    for r in range(tr):
        gpad[body, (r + 1) * cols : (r + 2) * cols] = g_ref[r].reshape(T * cout, cols)
    below = halo_ref[1].reshape(T * cout, cols)
    gpad[body, (tr + 1) * cols :] = jnp.where(me == 2 * W - 1, jnp.zeros_like(below), below)

    gsum[...] = jnp.zeros_like(gsum)
    tsum[...] = jnp.zeros_like(tsum)
    rows6 = tr + 4
    lane = lax.broadcasted_iota(jnp.int32, (rows6 * cin, cols), 1)
    lane_out = lax.broadcasted_iota(jnp.int32, (cin, cols), 1)
    bias = sb_ref[...]

    def frame(f, taps_mat, k_rows, g_start):
        x = slab_ref[f].reshape(rows6 * cin, cols)
        xf = x.astype(F32)
        left = jnp.where(lane == 0, 0.0, pltpu.roll(xf, 1, 1)).astype(BF16)
        right = jnp.where(lane == cols - 1, 0.0, pltpu.roll(xf, cols - 1, 1)).astype(BF16)
        stack[:, 0] = left.reshape(rows6, cin, cols)
        stack[:, 1] = x.reshape(rows6, cin, cols)
        stack[:, 2] = right.reshape(rows6, cin, cols)
        big = jnp.concatenate(
            [stack[r : r + 3].reshape(9 * cin, cols) for r in range(gp_rows)], axis=1
        )
        pre = jnp.dot(ws_ref[...], big, preferred_element_type=F32) + bias
        s = 1.0 / (1.0 + jnp.exp(-pre))
        act = (pre[:, cols : cols + px] * s[:, cols : cols + px]).astype(BF16)
        apad[pl.ds(pl.multiple_of((f + half) * cmid, 16), cmid), :] = act
        ga = jnp.dot(
            taps_mat, gpad[pl.ds(pl.multiple_of(g_start, 16), k_rows), :], preferred_element_type=F32
        )
        slope = s * (1.0 + pre * (1.0 - s))
        gp = (ga.astype(BF16).astype(F32) * slope).astype(BF16)
        gsum[...] += nt(gp[:, cols : cols + px], big[:, cols : cols + px])
        tall = jnp.concatenate([gp[:, i * cols : i * cols + px] for i in range(3)], axis=0)
        z = jnp.dot(wv_ref[...], tall, preferred_element_type=F32)
        for r in range(tr):
            zr = z[:, r * cols : (r + 1) * cols]
            total = zr[cin : 2 * cin]
            total += jnp.where(lane_out == cols - 1, 0.0, pltpu.roll(zr[0:cin], cols - 1, 1))
            total += jnp.where(lane_out == 0, 0.0, pltpu.roll(zr[2 * cin :], 1, 1))
            gv_ref[f, r] = total.astype(BF16)

    def pair(q, carry):
        frame(2 * q, we_ref[...], we_ref.shape[1], q * cout)
        frame(2 * q + 1, wo_ref[...], wo_ref.shape[1], (q + 1) * cout)
        return carry

    lax.fori_loop(0, F // 2, pair, 0)

    def step(t, carry):
        a = apad[pl.ds(pl.multiple_of(2 * t * cmid, 16), taps * cmid), :]
        o = jnp.dot(wt_ref[...], a, preferred_element_type=F32) + tb_ref[...]
        out_ref[t] = o.astype(BF16)
        g = gpad[pl.ds(pl.multiple_of((t + lead) * cout, 16), cout), cols : cols + px]
        tsum[...] += nt(g, a)
        return carry

    lax.fori_loop(0, T, step, 0)
    gs_ref[...] = gsum[...] * pscale
    gt_ref[...] = tsum[...] * tscale


def reduce_kernel(W, tr, part_ref, gv_ref, full_ref, gvr_ref,
                  nrecv, sbuf, rbuf, ns, nr, rs_s, rs_r, ag_s, ag_r, fw_s, fw_r, gv_s, gv_r, lsem):
    w = lax.axis_index("wide")
    n = lax.axis_index("narrow")
    per = W // 2
    goal = w // per
    greet_all(W)
    swap = remote(part_ref.at[1 - n], nrecv, ns, nr, w, 1 - n)
    swap.start()
    spot = lax.rem(w, per) * 2 + n

    def gv_copy(f):
        return remote(gv_ref.at[f], gvr_ref.at[pl.ds(spot * tr, tr)], gv_s.at[f], gv_r.at[spot], f, goal)

    swap.wait_recv()
    sbuf[...] = (part_ref[n] + nrecv[...]).astype(BF16)

    def rs_copy(dst):
        return remote(sbuf.at[dst], rbuf.at[w], rs_s.at[dst], rs_r.at[w], dst, n)

    def start_rs(k, carry):
        rs_copy(lax.rem(w + k, W)).start()
        return carry

    lax.fori_loop(1, W, start_rs, 0)

    def start_gv(k, carry):
        gv_copy(lax.rem(w + k, W)).start()
        return carry

    lax.fori_loop(1, W, start_gv, 0)

    mine = pltpu.make_async_copy(gv_ref.at[w], gvr_ref.at[pl.ds(spot * tr, tr)], lsem)

    @pl.when(goal == n)
    def _():
        mine.start()

    @pl.when(goal != n)
    def _():
        gv_copy(w).start()

    rbuf[w] = sbuf[w]

    def wait_rs(k, carry):
        src = lax.rem(w + W - k, W)
        remote(sbuf.at[src], rbuf.at[src], rs_s.at[src], rs_r.at[src], src, n).wait_recv()
        return carry

    lax.fori_loop(1, W, wait_rs, 0)
    full_ref[n, w] = jnp.sum(rbuf[...].astype(F32), axis=0).astype(BF16)

    def ag_copy(dst):
        return remote(full_ref.at[n, w], full_ref.at[n, w], ag_s.at[dst], ag_r.at[w], dst, n)

    def start_ag(k, carry):
        ag_copy(lax.rem(w + k, W)).start()
        return carry

    lax.fori_loop(1, W, start_ag, 0)

    def fw_copy(src):
        return remote(full_ref.at[n, src], full_ref.at[n, src], fw_s.at[src], fw_r.at[src], w, 1 - n)

    fw_copy(w).start()

    def relay(k, carry):
        src = lax.rem(w + W - k, W)
        remote(full_ref.at[n, src], full_ref.at[n, src], ag_s.at[src], ag_r.at[src], src, n).wait_recv()
        fw_copy(src).start()
        return carry

    lax.fori_loop(1, W, relay, 0)

    first = per * 2 * n
    me = w * 2 + n

    def wait_gv(i, carry):
        @pl.when(first + i != me)
        def _():
            remote(
                gv_ref.at[0], gvr_ref.at[pl.ds(i * tr, tr)], gv_s.at[0], gv_r.at[i], w, 1 - n
            ).wait_recv()

        return carry

    lax.fori_loop(0, 2 * per, wait_gv, 0)

    def finish(k, carry):
        other = lax.rem(w + k, W)
        rs_copy(other).wait_send()
        ag_copy(other).wait_send()
        gv_copy(other).wait_send()
        return carry

    lax.fori_loop(1, W, finish, 0)

    def finish_fw(s, carry):
        remote(
            full_ref.at[1 - n, s], full_ref.at[1 - n, s], fw_s.at[s], fw_r.at[s], w, 1 - n
        ).wait_recv()
        fw_copy(s).wait_send()
        return carry

    lax.fori_loop(0, W, finish_fw, 0)
    swap.wait_send()

    @pl.when(goal == n)
    def _():
        mine.wait()

    @pl.when(goal != n)
    def _():
        gv_copy(w).wait_send()


def per_device(video, spatial_weight, spatial_bias, temporal_weight, temporal_bias, out_cotangent):
    W = lax.axis_size("wide")
    _, cin, R, cols = video.shape
    cmid = spatial_weight.shape[0]
    cout, taps, _ = temporal_weight.shape
    T = out_cotangent.shape[0]
    tr = out_cotangent.shape[2]
    F = W
    px = tr * cols
    half = taps // 2
    tscale = 1.0 / math.sqrt(T * R * cols)
    pscale = 1.0 / math.sqrt(F * R * cols)
    dma = pltpu.SemaphoreType.DMA
    hbm = pl.BlockSpec(memory_space=pl.ANY)
    vmem = pl.BlockSpec(memory_space=pltpu.VMEM)

    v_rows = jnp.pad(jnp.transpose(video[0], (1, 0, 2)), ((2, 2), (0, 0), (0, 0)))
    g_rows = jnp.transpose(out_cotangent, (2, 0, 1, 3))
    slab, halo = pl.pallas_call(
        functools.partial(gather_kernel, W, tr),
        out_shape=(
            jax.ShapeDtypeStruct((F, tr + 4, cin, cols), BF16),
            jax.ShapeDtypeStruct((2, T, cout, cols), BF16),
        ),
        in_specs=[hbm, hbm],
        out_specs=(hbm, hbm),
        scratch_shapes=[dma((W,)), dma((W,)), dma((W,)), dma((W,)), dma((2,)), dma((2,)), dma],
        compiler_params=pltpu.CompilerParams(collective_id=0, has_side_effects=True),
        name="gather_rows",
    )(v_rows, g_rows)

    ws = spatial_weight.reshape(cmid, 9 * cin)
    grid_w = spatial_weight.reshape(cmid, 3, 3, cin)[:, ::-1]
    wv = jnp.transpose(grid_w, (2, 3, 1, 0)).reshape(3 * cin, 3 * cmid)
    wt = temporal_weight.reshape(cout, taps * cmid)
    rev = jnp.transpose(temporal_weight[:, ::-1], (2, 1, 0))
    we = rev[:, 0::2].reshape(cmid, -1)
    wo = rev[:, 1::2].reshape(cmid, -1)

    out, gv, gs, gt = pl.pallas_call(
        functools.partial(compute_kernel, W, tr, F, T, taps, pscale, tscale),
        out_shape=(
            jax.ShapeDtypeStruct((T, cout, px), BF16),
            jax.ShapeDtypeStruct((F, tr, cin, cols), BF16),
            jax.ShapeDtypeStruct((cmid, 9 * cin), F32),
            jax.ShapeDtypeStruct((cout, taps * cmid), F32),
        ),
        in_specs=[vmem] * 10,
        out_specs=(vmem,) * 4,
        scratch_shapes=[
            pltpu.VMEM((tr + 4, 3, cin, cols), BF16),
            pltpu.VMEM(((T + half) * cout, (tr + 2) * cols), BF16),
            pltpu.VMEM(((F + 2 * half) * cmid, px), BF16),
            pltpu.VMEM((cmid, 9 * cin), F32),
            pltpu.VMEM((cout, taps * cmid), F32),
        ],
        compiler_params=pltpu.CompilerParams(vmem_limit_bytes=VMEM_BYTES),
        name="block_compute",
    )(slab, g_rows, halo, ws, spatial_bias[:, None], wv, wt, temporal_bias[:, None], we, wo)

    size_s = cmid * 9 * cin // 2
    size_t = cout * taps * cmid // 2
    rows = -(-(size_s + size_t) // (W * 128 * 16)) * 16
    flat = jnp.concatenate([gs.reshape(2, size_s), gt.reshape(2, size_t)], axis=1)
    flat = jnp.pad(flat, ((0, 0), (0, W * rows * 128 - size_s - size_t)))
    full, gv_rows = pl.pallas_call(
        functools.partial(reduce_kernel, W, tr),
        out_shape=(
            jax.ShapeDtypeStruct((2, W, rows, 128), BF16),
            jax.ShapeDtypeStruct((R // 2, cin, cols), BF16),
        ),
        in_specs=[vmem, hbm],
        out_specs=(vmem, hbm),
        scratch_shapes=[
            pltpu.VMEM((W, rows, 128), F32),
            pltpu.VMEM((W, rows, 128), BF16),
            pltpu.VMEM((W, rows, 128), BF16),
            dma, dma, dma((W,)), dma((W,)), dma((W,)), dma((W,)), dma((W,)), dma((W,)), dma((W,)), dma((W,)), dma,
        ],
        compiler_params=pltpu.CompilerParams(
            collective_id=1, has_side_effects=True, vmem_limit_bytes=VMEM_BYTES
        ),
        name="reduce_and_return",
    )(flat.reshape(2, W, rows, 128), gv)

    full = full.reshape(2, W * rows * 128)
    own = lax.dynamic_index_in_dim(full, lax.axis_index("narrow"), 0, keepdims=False)
    grad_spatial = own[:size_s].reshape(cmid // 2, 9, cin).astype(F32)
    grad_temporal = full[:, size_s : size_s + size_t].reshape(cout, taps, cmid).astype(F32)
    grad_video = jnp.transpose(gv_rows, (1, 0, 2))[None]
    output = out.reshape(T, cout, tr, cols)
    return (output, grad_video, grad_spatial, grad_temporal)


def solution(mesh):
    in_specs = (
        P(("grp", "wide"), None, None, None),
        P(),
        P(),
        P(),
        P(),
        P("grp", None, ("wide", "narrow"), None),
    )
    out_specs = (
        P("grp", None, ("wide", "narrow"), None),
        P(("grp", "wide"), None, "narrow", None),
        P(("grp", "narrow"), None, None),
        P("grp", None, None),
    )
    return jax.shard_map(
        per_device, mesh=mesh, in_specs=in_specs, out_specs=out_specs, check_vma=False
    )
```

```python
import functools
import math

import jax
import jax.numpy as jnp
from jax import lax
from jax.experimental import pallas as pl
from jax.experimental.pallas import tpu as pltpu
from jax.sharding import PartitionSpec as P

MESH = pl.DeviceIdType.MESH
BF16 = jnp.bfloat16
F32 = jnp.float32
VMEM_BYTES = 50 * 1024 * 1024


def greet_all(wide_count):
    me = lax.axis_index("wide") * 2 + lax.axis_index("narrow")
    total = 2 * wide_count
    barrier = pltpu.get_barrier_semaphore()

    def greet(k, carry):
        other = lax.rem(me + k, total)
        pl.semaphore_signal(
            barrier, inc=1, device_id={"wide": other // 2, "narrow": lax.rem(other, 2)}, device_id_type=MESH
        )
        return carry

    lax.fori_loop(1, total, greet, 0)
    pl.semaphore_wait(barrier, total - 1)


def remote(src, dst, send_sem, recv_sem, wide, narrow):
    return pltpu.make_async_remote_copy(
        src_ref=src,
        dst_ref=dst,
        send_sem=send_sem,
        recv_sem=recv_sem,
        device_id={"wide": wide, "narrow": narrow},
        device_id_type=MESH,
    )


def nt(a, b):
    return lax.dot_general(a, b, (((1,), (1,)), ((), ())), preferred_element_type=F32)


def fold_lanes(x):
    rows, lanes = x.shape
    blocks = lanes // 128
    parts = [x[:, 128 * b : 128 * (b + 1)] for b in range(blocks)]
    left = lanes - 128 * blocks
    if not left:
        return parts, []
    fold = 128 // left
    piece = rows // fold
    last = jnp.concatenate([x[piece * i : piece * (i + 1), 128 * blocks :] for i in range(fold)], axis=1)
    return parts, [last]


def unfold_lanes(parts, last, lanes):
    blocks = lanes // 128
    left = lanes - 128 * blocks
    if not left:
        return jnp.concatenate(parts, axis=1)
    fold = 128 // left
    end = jnp.concatenate([last[:, left * i : left * (i + 1)] for i in range(fold)], axis=0)
    return jnp.concatenate(parts + [end], axis=1)


def block_kernel(
    W, tr, T, taps, rows, pscale, tscale,
    v_ref, g_ref, ws_ref, sb_ref, wt_ref, tb_ref,
    out_ref, gvr_ref, gs_ref, gt_ref,
    vpad, slab, halo, stack, gpad, apad, gsum, tsum, wv, wtap, gv,
    nrs, nrt, sbuf, rbuf, full,
    v_s, v_r, vf_s, vf_r, h_s, h_r, ns, nr, rs_s, rs_r, ag_s, ag_r, fw_s, fw_r, gv_s, gv_r, lsem,
):
    F = W
    w = lax.axis_index("wide")
    n = lax.axis_index("narrow")
    me = w * 2 + n
    R, cin, cols = v_ref.shape
    cmid = ws_ref.shape[0]
    cout = wt_ref.shape[0]
    half = taps // 2
    lead = half // 2
    gp_rows = tr + 2
    px = tr * cols
    rows6 = tr + 4
    got = tr + 2
    even_taps = half + 1
    per = W // 2
    goal = w // per
    spot = lax.rem(w, per) * 2 + n
    low_tap = 2 * (T - 1) - half
    place = 2 * n

    vpad[0:2] = jnp.zeros((2, cin, cols), BF16)
    vpad[R + 2 :] = jnp.zeros((2, cin, cols), BF16)
    vpad[2 : R + 2] = v_ref[...]
    greet_all(W)

    nxt = lax.rem(me + 1, 2 * W)
    prv = lax.rem(me + 2 * W - 1, 2 * W)
    down = remote(g_ref.at[tr - 1], halo.at[0], h_s.at[0], h_r.at[0], nxt // 2, lax.rem(nxt, 2))
    up = remote(g_ref.at[0], halo.at[1], h_s.at[1], h_r.at[1], prv // 2, lax.rem(prv, 2))
    down.start()
    up.start()

    def v_copy(dst):
        return remote(
            vpad.at[pl.ds(2 * tr * dst + got * n, got)], slab.at[w, pl.ds(place, got)], v_s.at[dst], v_r.at[w], dst, n
        )

    def v_arrival(src):
        return remote(
            vpad.at[pl.ds(0, got)], slab.at[src, pl.ds(place, got)], v_s.at[src], v_r.at[src], src, n
        )

    def v_forward(src):
        return remote(
            slab.at[src, pl.ds(tr * (1 - n) + 2 * n, 2)], slab.at[src, pl.ds(got * n, 2)],
            vf_s.at[src], vf_r.at[src], w, 1 - n,
        )

    def v_forwarded(src):
        return remote(
            slab.at[src, pl.ds(0, 2)], slab.at[src, pl.ds(got * (1 - n), 2)], vf_s.at[src], vf_r.at[src], w, 1 - n
        )

    def gv_copy(f):
        return remote(gv.at[f], gvr_ref.at[pl.ds(spot * tr, tr)], gv_s.at[f], gv_r.at[spot], f, goal)

    mine = pltpu.make_async_copy(gv.at[w], gvr_ref.at[pl.ds(spot * tr, tr)], lsem)

    def start(k, carry):
        v_copy(lax.rem(w + k, W)).start()
        return carry

    lax.fori_loop(1, W, start, 0)

    slab[w] = vpad[pl.ds(2 * tr * w + tr * n, rows6)]
    for i in range(3):
        wv[i] = ws_ref[:, 3 * cin * i : 3 * cin * (i + 1)].astype(F32).T.astype(BF16)
    for parity in range(2):
        for m in range(even_taps):
            k = taps - 1 - parity - 2 * m
            spread = slice(m * cout, (m + 1) * cout)
            if k < 0:
                wtap[parity, :, spread] = jnp.zeros((cmid, cout), BF16)
            else:
                wtap[parity, :, spread] = wt_ref[:, k * cmid : (k + 1) * cmid].astype(F32).T.astype(BF16)
    gpad[0 : lead * cout, :] = jnp.zeros((lead * cout, gp_rows * cols), BF16)
    gpad[(lead + T) * cout :, :] = jnp.zeros(((lead + 1) * cout, gp_rows * cols), BF16)
    apad[0 : half * cmid, :] = jnp.zeros((half * cmid, px), BF16)
    apad[(half + F) * cmid :, :] = jnp.zeros((half * cmid, px), BF16)
    gsum[...] = jnp.zeros_like(gsum)
    tsum[...] = jnp.zeros_like(tsum)

    body = slice(lead * cout, (lead + T) * cout)
    for r in range(tr):
        gpad[body, (r + 1) * cols : (r + 2) * cols] = g_ref[r].reshape(T * cout, cols)
    down.wait_recv()
    up.wait_recv()
    above = halo[0].reshape(T * cout, cols)
    gpad[body, 0:cols] = jnp.where(me == 0, jnp.zeros_like(above), above)
    below = halo[1].reshape(T * cout, cols)
    gpad[body, (tr + 1) * cols :] = jnp.where(me == 2 * W - 1, jnp.zeros_like(below), below)

    lane = lax.broadcasted_iota(jnp.int32, (rows6 * cin, cols), 1)
    lane_out = lax.broadcasted_iota(jnp.int32, (cin, cols), 1)

    def frame(f):
        x = slab[f].reshape(rows6 * cin, cols)
        xf = x.astype(F32)
        left = jnp.where(lane == 0, 0.0, pltpu.roll(xf, 1, 1)).astype(BF16)
        right = jnp.where(lane == cols - 1, 0.0, pltpu.roll(xf, cols - 1, 1)).astype(BF16)
        stack[:, 0] = left.reshape(rows6, cin, cols)
        stack[:, 1] = x.reshape(rows6, cin, cols)
        stack[:, 2] = right.reshape(rows6, cin, cols)
        big = jnp.concatenate(
            [stack[r : r + 3].reshape(9 * cin, cols) for r in range(gp_rows)], axis=1
        )
        pre = jnp.dot(ws_ref[...], big, preferred_element_type=F32) + sb_ref[...]
        s = 1.0 / (1.0 + jnp.exp(-pre))
        act = (pre[:, cols : cols + px] * s[:, cols : cols + px]).astype(BF16)
        apad[pl.ds(pl.multiple_of((f + half) * cmid, 16), cmid), :] = act
        odd = lax.rem(f, 2)
        g_start = pl.multiple_of((f // 2 + odd) * cout, 16)
        ga = jnp.dot(wtap[odd], gpad[pl.ds(g_start, even_taps * cout), :], preferred_element_type=F32)
        slope = s * (1.0 + pre * (1.0 - s))
        gp = (ga.astype(BF16).astype(F32) * slope).astype(BF16)
        z = jnp.dot(wv[2], gp[:, 0:px], preferred_element_type=F32)
        z += jnp.dot(wv[1], gp[:, cols : cols + px], preferred_element_type=F32)
        z += jnp.dot(wv[0], gp[:, 2 * cols : 2 * cols + px], preferred_element_type=F32)
        for r in range(tr):
            zr = z[:, r * cols : (r + 1) * cols]
            total = zr[cin : 2 * cin]
            total += jnp.where(lane_out == cols - 1, 0.0, pltpu.roll(zr[0:cin], cols - 1, 1))
            total += jnp.where(lane_out == 0, 0.0, pltpu.roll(zr[2 * cin :], 1, 1))
            gv[f, r] = total.astype(BF16)
        gsum[...] += nt(gp[:, cols : cols + px], big[:, cols : cols + px])
        pairs = nt(gpad[body, cols : cols + px], act)
        for t in range(T):
            at = f + 2 * (T - 1 - t)
            tsum[at] += pairs[t * cout : (t + 1) * cout]

    frame(w)

    @pl.when(goal == n)
    def _():
        mine.start()

    @pl.when(goal != n)
    def _():
        gv_copy(w).start()

    v_arrival(lax.rem(w + W - 1, W)).wait_recv()
    v_forward(lax.rem(w + W - 1, W)).start()

    def each(k, carry):
        src = lax.rem(w + W - k, W)
        after = lax.rem(w + W - k - 1, W)

        @pl.when(k < W - 1)
        def _():
            v_arrival(after).wait_recv()
            v_forward(after).start()

        v_forwarded(src).wait_recv()
        frame(src)
        gv_copy(src).start()
        return carry

    lax.fori_loop(1, W, each, 0)

    hs, ht = cmid // 2, cout // 2

    def half_of(ref, size, which):
        return ref.at[pl.ds(pl.multiple_of(which * size, 8), size)]

    def tap_half(which):
        return tsum.at[pl.ds(low_tap, taps), pl.ds(pl.multiple_of(which * ht, 8), ht)]

    swap_s = remote(half_of(gsum, hs, 1 - n), nrs, ns.at[0], nr.at[0], w, 1 - n)
    swap_t = remote(tap_half(1 - n), nrt, ns.at[1], nr.at[1], w, 1 - n)
    swap_s.start()
    swap_t.start()
    swap_s.wait_recv()
    swap_t.wait_recv()
    mine_s = (gsum[pl.ds(pl.multiple_of(n * hs, 8), hs), :] + nrs[...]) * pscale
    mine_t = (tsum[pl.ds(low_tap, taps), pl.ds(pl.multiple_of(n * ht, 8), ht), :] + nrt[...]) * tscale
    main_s, last_s = fold_lanes(mine_s)
    main_t, last_t = fold_lanes(mine_t.reshape(taps * ht, cmid))
    flat = jnp.concatenate(main_s + main_t + last_s + last_t, axis=0)
    used = flat.shape[0]
    flat = jnp.concatenate([flat, jnp.zeros((W * rows - used, 128), F32)], axis=0)
    sbuf[...] = flat.astype(BF16)

    def chunk(i):
        return pl.ds(pl.multiple_of(i * rows, 16), rows)

    def rs_copy(dst):
        return remote(sbuf.at[chunk(dst)], rbuf.at[w], rs_s.at[dst], rs_r.at[w], dst, n)

    def start_rs(k, carry):
        rs_copy(lax.rem(w + k, W)).start()
        return carry

    lax.fori_loop(1, W, start_rs, 0)
    rbuf[w] = sbuf[chunk(w), :]

    def step(t, carry):
        a = apad[pl.ds(pl.multiple_of(2 * t * cmid, 16), taps * cmid), :]
        o = jnp.dot(wt_ref[...], a, preferred_element_type=F32) + tb_ref[...]
        out_ref[t] = o.astype(BF16)
        return carry

    lax.fori_loop(0, T, step, 0)

    def wait_rs(k, carry):
        src = lax.rem(w + W - k, W)
        remote(sbuf.at[chunk(src)], rbuf.at[src], rs_s.at[src], rs_r.at[src], src, n).wait_recv()
        return carry

    lax.fori_loop(1, W, wait_rs, 0)
    full[n, chunk(w), :] = jnp.sum(rbuf[...].astype(F32), axis=0).astype(BF16)

    def ag_copy(dst):
        return remote(full.at[n, chunk(w)], full.at[n, chunk(w)], ag_s.at[dst], ag_r.at[w], dst, n)

    def start_ag(k, carry):
        ag_copy(lax.rem(w + k, W)).start()
        return carry

    lax.fori_loop(1, W, start_ag, 0)

    def fw_copy(src):
        return remote(full.at[n, chunk(src)], full.at[n, chunk(src)], fw_s.at[src], fw_r.at[src], w, 1 - n)

    fw_copy(w).start()

    def relay(k, carry):
        src = lax.rem(w + W - k, W)
        remote(full.at[n, chunk(src)], full.at[n, chunk(src)], ag_s.at[src], ag_r.at[src], src, n).wait_recv()
        fw_copy(src).start()
        return carry

    lax.fori_loop(1, W, relay, 0)

    first = per * 2 * n

    def wait_gv(i, carry):
        @pl.when(first + i != me)
        def _():
            remote(gv.at[0], gvr_ref.at[pl.ds(i * tr, tr)], gv_s.at[0], gv_r.at[i], w, 1 - n).wait_recv()

        return carry

    lax.fori_loop(0, 2 * per, wait_gv, 0)

    def finish(k, carry):
        other = lax.rem(w + k, W)
        v_copy(other).wait_send()
        v_forward(other).wait_send()
        rs_copy(other).wait_send()
        ag_copy(other).wait_send()
        gv_copy(other).wait_send()
        return carry

    lax.fori_loop(1, W, finish, 0)

    def finish_fw(s, carry):
        remote(
            full.at[1 - n, chunk(s)], full.at[1 - n, chunk(s)], fw_s.at[s], fw_r.at[s], w, 1 - n
        ).wait_recv()
        fw_copy(s).wait_send()
        return carry

    lax.fori_loop(0, W, finish_fw, 0)
    down.wait_send()
    up.wait_send()
    swap_s.wait_send()
    swap_t.wait_send()

    @pl.when(goal == n)
    def _():
        mine.wait()

    @pl.when(goal != n)
    def _():
        gv_copy(w).wait_send()

    def spans(base, count, size):
        return [slice(base + i * size, base + (i + 1) * size) for i in range(count)]

    ns_blocks, nt_blocks = len(main_s), len(main_t)
    base_t = ns_blocks * hs
    base_ls = base_t + nt_blocks * taps * ht
    base_lt = base_ls + (last_s[0].shape[0] if last_s else 0)
    whole = full[n].astype(F32)
    gs_ref[...] = unfold_lanes(
        [whole[c] for c in spans(0, ns_blocks, hs)], whole[base_ls:base_lt], ws_ref.shape[1]
    )
    for h in range(2):
        whole = full[h].astype(F32)
        taps_h = unfold_lanes(
            [whole[c] for c in spans(base_t, nt_blocks, taps * ht)], whole[base_lt:used], cmid
        )
        gt_ref[:, h * ht : (h + 1) * ht, :] = taps_h.reshape(taps, ht, cmid)


def per_device(video, spatial_weight, spatial_bias, temporal_weight, temporal_bias, out_cotangent):
    W = lax.axis_size("wide")
    _, cin, R, cols = video.shape
    cmid = spatial_weight.shape[0]
    cout, taps, _ = temporal_weight.shape
    T = out_cotangent.shape[0]
    tr = out_cotangent.shape[2]
    F = W
    px = tr * cols
    half = taps // 2
    tscale = 1.0 / math.sqrt(T * R * cols)
    pscale = 1.0 / math.sqrt(F * R * cols)
    dma = pltpu.SemaphoreType.DMA
    vmem = pl.BlockSpec(memory_space=pltpu.VMEM)
    words = (cmid * 9 * cin + cout * taps * cmid) // 2
    rows = -(-words // (W * 128 * 16)) * 16

    v_rows = jnp.transpose(video[0], (1, 0, 2))
    g_rows = jnp.transpose(out_cotangent, (2, 0, 1, 3))
    ws = spatial_weight.reshape(cmid, 9 * cin)
    wt = temporal_weight.reshape(cout, taps * cmid)

    out, gv_rows, gs, gt = pl.pallas_call(
        functools.partial(block_kernel, W, tr, T, taps, rows, pscale, tscale),
        out_shape=(
            jax.ShapeDtypeStruct((T, cout, px), BF16),
            jax.ShapeDtypeStruct((R // 2, cin, cols), BF16),
            jax.ShapeDtypeStruct((cmid // 2, 9 * cin), F32),
            jax.ShapeDtypeStruct((taps, cout, cmid), F32),
        ),
        in_specs=[vmem] * 6,
        out_specs=(vmem,) * 4,
        scratch_shapes=[
            pltpu.VMEM((R + 4, cin, cols), BF16),
            pltpu.VMEM((F, tr + 4, cin, cols), BF16),
            pltpu.VMEM((2, T, cout, cols), BF16),
            pltpu.VMEM((tr + 4, 3, cin, cols), BF16),
            pltpu.VMEM(((T + half + 1) * cout, (tr + 2) * cols), BF16),
            pltpu.VMEM(((F + 2 * half) * cmid, px), BF16),
            pltpu.VMEM((cmid, 9 * cin), F32),
            pltpu.VMEM((F + 2 * (T - 1), cout, cmid), F32),
            pltpu.VMEM((3, 3 * cin, cmid), BF16),
            pltpu.VMEM((2, cmid, (half + 1) * cout), BF16),
            pltpu.VMEM((F, tr, cin, cols), BF16),
            pltpu.VMEM((cmid // 2, 9 * cin), F32),
            pltpu.VMEM((taps, cout // 2, cmid), F32),
            pltpu.VMEM((W * rows, 128), BF16),
            pltpu.VMEM((W, rows, 128), BF16),
            pltpu.VMEM((2, W * rows, 128), BF16),
        ]
        + [dma((W,))] * 4
        + [dma((2,))] * 4
        + [dma((W,))] * 8
        + [dma],
        compiler_params=pltpu.CompilerParams(
            collective_id=0, has_side_effects=True, vmem_limit_bytes=VMEM_BYTES
        ),
        name="space_time_block",
    )(v_rows, g_rows, ws, spatial_bias[:, None], wt, temporal_bias[:, None])

    grad_spatial = gs.reshape(cmid // 2, 9, cin)
    grad_temporal = jnp.transpose(gt, (1, 0, 2))
    grad_video = jnp.transpose(gv_rows, (1, 0, 2))[None]
    output = out.reshape(T, cout, tr, cols)
    return (output, grad_video, grad_spatial, grad_temporal)


def solution(mesh):
    in_specs = (
        P(("grp", "wide"), None, None, None),
        P(),
        P(),
        P(),
        P(),
        P("grp", None, ("wide", "narrow"), None),
    )
    out_specs = (
        P("grp", None, ("wide", "narrow"), None),
        P(("grp", "wide"), None, "narrow", None),
        P(("grp", "narrow"), None, None),
        P("grp", None, None),
    )
    return jax.shard_map(
        per_device, mesh=mesh, in_specs=in_specs, out_specs=out_specs, check_vma=False
    )
```

```python
import functools
import math

import jax
import jax.numpy as jnp
from jax import lax
from jax.experimental import pallas as pl
from jax.experimental.pallas import tpu as pltpu
from jax.sharding import PartitionSpec as P

MESH = pl.DeviceIdType.MESH
BF16 = jnp.bfloat16
F32 = jnp.float32
LAG = 2
VMEM_BYTES = 50 * 1024 * 1024


def greet_all(wide_count, between):
    me = lax.axis_index("wide") * 2 + lax.axis_index("narrow")
    total = 2 * wide_count
    barrier = pltpu.get_barrier_semaphore()

    def greet(k, carry):
        other = lax.rem(me + k, total)
        pl.semaphore_signal(
            barrier, inc=1, device_id={"wide": other // 2, "narrow": lax.rem(other, 2)}, device_id_type=MESH
        )
        return carry

    lax.fori_loop(1, total, greet, 0)
    between()
    pl.semaphore_wait(barrier, total - 1)


def remote(src, dst, send_sem, recv_sem, wide, narrow):
    return pltpu.make_async_remote_copy(
        src_ref=src,
        dst_ref=dst,
        send_sem=send_sem,
        recv_sem=recv_sem,
        device_id={"wide": wide, "narrow": narrow},
        device_id_type=MESH,
    )


def nt(a, b):
    return lax.dot_general(a, b, (((1,), (1,)), ((), ())), preferred_element_type=F32)


def fold_lanes(x):
    rows, lanes = x.shape
    blocks = lanes // 128
    parts = [x[:, 128 * b : 128 * (b + 1)] for b in range(blocks)]
    left = lanes - 128 * blocks
    if not left:
        return parts, []
    fold = 128 // left
    piece = rows // fold
    last = jnp.concatenate([x[piece * i : piece * (i + 1), 128 * blocks :] for i in range(fold)], axis=1)
    return parts, [last]


def unfold_lanes(parts, last, lanes):
    blocks = lanes // 128
    left = lanes - 128 * blocks
    if not left:
        return jnp.concatenate(parts, axis=1)
    fold = 128 // left
    end = jnp.concatenate([last[:, left * i : left * (i + 1)] for i in range(fold)], axis=0)
    return jnp.concatenate(parts + [end], axis=1)


def block_kernel(
    W, tr, T, taps, rows, pscale, tscale,
    v_ref, g_ref, ws_ref, sb_ref, wt_ref, tb_ref,
    out_ref, gvr_ref, gs_ref, gt_ref,
    slab, halo, stack, gpad, apad, gsum, tsum, wv, wtap, gv,
    nrs, nrt, sbuf, rbuf, full,
    v_s, v_r, vd_s, vd_r, vu_s, vu_r, h_s, h_r, ns, nr, rs_s, rs_r, ag_s, ag_r, fw_s, fw_r, gv_s, gv_r, lsem,
):
    F = W
    w = lax.axis_index("wide")
    n = lax.axis_index("narrow")
    me = w * 2 + n
    R, cin, cols = v_ref.shape
    cmid = ws_ref.shape[0]
    cout = wt_ref.shape[0]
    half = taps // 2
    lead = half // 2
    gp_rows = tr + 2
    px = tr * cols
    rows6 = tr + 4
    even_taps = half + 1
    per = W // 2
    goal = w // per
    spot = lax.rem(w, per) * 2 + n
    low_tap = 2 * (T - 1) - half

    def between():
        for i in range(3):
            wv[i] = ws_ref[:, 3 * cin * i : 3 * cin * (i + 1)].astype(F32).T.astype(BF16)

    greet_all(W, between)

    nxt = lax.rem(me + 1, 2 * W)
    prv = lax.rem(me + 2 * W - 1, 2 * W)
    down = remote(g_ref.at[tr - 1], halo.at[0], h_s.at[0], h_r.at[0], nxt // 2, lax.rem(nxt, 2))
    up = remote(g_ref.at[0], halo.at[1], h_s.at[1], h_r.at[1], prv // 2, lax.rem(prv, 2))
    down.start()
    up.start()

    def v_copy(dst):
        return remote(
            v_ref.at[pl.ds(2 * tr * dst + tr * n, tr)], slab.at[w, pl.ds(2, tr)], v_s.at[dst], v_r.at[w], dst, n
        )

    def v_arrival(src):
        return remote(v_ref.at[pl.ds(0, tr)], slab.at[src, pl.ds(2, tr)], v_s.at[src], v_r.at[src], src, n)

    def to_next(src):
        return remote(
            slab.at[src, pl.ds(tr, 2)], slab.at[src, pl.ds(0, 2)], vd_s.at[src], vd_r.at[src], nxt // 2, 1 - n
        )

    def to_prev(src):
        return remote(
            slab.at[src, pl.ds(2, 2)], slab.at[src, pl.ds(tr + 2, 2)], vu_s.at[src], vu_r.at[src], prv // 2, 1 - n
        )

    sends_down = me < 2 * W - 1
    sends_up = me > 0

    def hand_on(src, act):
        @pl.when(jnp.logical_and(sends_down, src != nxt // 2))
        def _():
            act(to_next(src))

        @pl.when(jnp.logical_and(sends_up, src != prv // 2))
        def _():
            act(to_prev(src))

    def await_halo(src):
        @pl.when(sends_up)
        def _():
            to_next(src).wait_recv()

        @pl.when(sends_down)
        def _():
            to_prev(src).wait_recv()

    def gv_copy(f):
        return remote(gv.at[f], gvr_ref.at[pl.ds(spot * tr, tr)], gv_s.at[f], gv_r.at[spot], f, goal)

    mine = pltpu.make_async_copy(gv.at[w], gvr_ref.at[pl.ds(spot * tr, tr)], lsem)

    def start(k, carry):
        v_copy(lax.rem(w + k, W)).start()
        return carry

    lax.fori_loop(1, W, start, 0)

    slab[w, 2 : 2 + tr] = v_ref[pl.ds(tr * me, tr)]
    hand_on(w, lambda copy: copy.start())
    edge = jnp.zeros((2, cin, cols), BF16)

    @pl.when(sends_up)
    def _():
        slab[w, 0:2] = v_ref[pl.ds(jnp.maximum(tr * me - 2, 0), 2)]

    @pl.when(sends_down)
    def _():
        slab[w, tr + 2 :] = v_ref[pl.ds(jnp.minimum(tr * me + tr, R - 2), 2)]

    @pl.when(jnp.logical_not(sends_up))
    def _():
        for f in range(F):
            slab[f, 0:2] = edge

    @pl.when(jnp.logical_not(sends_down))
    def _():
        for f in range(F):
            slab[f, tr + 2 :] = edge

    for parity in range(2):
        for m in range(even_taps):
            k = taps - 1 - parity - 2 * m
            spread = slice(m * cout, (m + 1) * cout)
            if k < 0:
                wtap[parity, :, spread] = jnp.zeros((cmid, cout), BF16)
            else:
                wtap[parity, :, spread] = wt_ref[:, k * cmid : (k + 1) * cmid].astype(F32).T.astype(BF16)
    gpad[0 : lead * cout, :] = jnp.zeros((lead * cout, gp_rows * cols), BF16)
    gpad[(lead + T) * cout :, :] = jnp.zeros(((lead + 1) * cout, gp_rows * cols), BF16)
    apad[0 : half * cmid, :] = jnp.zeros((half * cmid, px), BF16)
    apad[(half + F) * cmid :, :] = jnp.zeros((half * cmid, px), BF16)
    gsum[...] = jnp.zeros_like(gsum)
    tsum[...] = jnp.zeros_like(tsum)

    body = slice(lead * cout, (lead + T) * cout)
    for r in range(tr):
        gpad[body, (r + 1) * cols : (r + 2) * cols] = g_ref[r].reshape(T * cout, cols)
    down.wait_recv()
    up.wait_recv()
    above = halo[0].reshape(T * cout, cols)
    gpad[body, 0:cols] = jnp.where(me == 0, jnp.zeros_like(above), above)
    below = halo[1].reshape(T * cout, cols)
    gpad[body, (tr + 1) * cols :] = jnp.where(me == 2 * W - 1, jnp.zeros_like(below), below)

    sb = jnp.broadcast_to(sb_ref[...], (8, cmid)).T[:, 0:1]
    tb = jnp.broadcast_to(tb_ref[...], (8, cout)).T[:, 0:1]
    lane = lax.broadcasted_iota(jnp.int32, (rows6 * cin, cols), 1)
    lane_out = lax.broadcasted_iota(jnp.int32, (cin, cols), 1)

    def frame(f):
        x = slab[f].reshape(rows6 * cin, cols)
        xf = x.astype(F32)
        left = jnp.where(lane == 0, 0.0, pltpu.roll(xf, 1, 1)).astype(BF16)
        right = jnp.where(lane == cols - 1, 0.0, pltpu.roll(xf, cols - 1, 1)).astype(BF16)
        stack[:, 0] = left.reshape(rows6, cin, cols)
        stack[:, 1] = x.reshape(rows6, cin, cols)
        stack[:, 2] = right.reshape(rows6, cin, cols)
        big = jnp.concatenate(
            [stack[r : r + 3].reshape(9 * cin, cols) for r in range(gp_rows)], axis=1
        )
        pre = jnp.dot(ws_ref[...], big, preferred_element_type=F32) + sb
        s = 1.0 / (1.0 + jnp.exp(-pre))
        act = (pre[:, cols : cols + px] * s[:, cols : cols + px]).astype(BF16)
        apad[pl.ds(pl.multiple_of((f + half) * cmid, 16), cmid), :] = act
        odd = lax.rem(f, 2)
        g_start = pl.multiple_of((f // 2 + odd) * cout, 16)
        ga = jnp.dot(wtap[odd], gpad[pl.ds(g_start, even_taps * cout), :], preferred_element_type=F32)
        slope = s * (1.0 + pre * (1.0 - s))
        gp = (ga.astype(BF16).astype(F32) * slope).astype(BF16)
        z = jnp.dot(wv[2], gp[:, 0:px], preferred_element_type=F32)
        z += jnp.dot(wv[1], gp[:, cols : cols + px], preferred_element_type=F32)
        z += jnp.dot(wv[0], gp[:, 2 * cols : 2 * cols + px], preferred_element_type=F32)
        for r in range(tr):
            zr = z[:, r * cols : (r + 1) * cols]
            total = zr[cin : 2 * cin]
            total += jnp.where(lane_out == cols - 1, 0.0, pltpu.roll(zr[0:cin], cols - 1, 1))
            total += jnp.where(lane_out == 0, 0.0, pltpu.roll(zr[2 * cin :], 1, 1))
            gv[f, r] = total.astype(BF16)
        gsum[...] += nt(gp[:, cols : cols + px], big[:, cols : cols + px])
        pairs = nt(gpad[body, cols : cols + px], act)
        for t in range(T):
            at = f + 2 * (T - 1 - t)
            tsum[at] += pairs[t * cout : (t + 1) * cout]

    frame(w)

    @pl.when(goal == n)
    def _():
        mine.start()

    @pl.when(goal != n)
    def _():
        gv_copy(w).start()

    def take(k):
        src = lax.rem(w + 2 * W - k, W)
        v_arrival(src).wait_recv()
        hand_on(src, lambda copy: copy.start())

    for k in range(1, 1 + LAG):
        take(k)

    def each(k, carry):
        src = lax.rem(w + W - k, W)

        @pl.when(k < W - LAG)
        def _():
            take(k + LAG)

        await_halo(src)
        frame(src)
        gv_copy(src).start()
        return carry

    lax.fori_loop(1, W, each, 0)

    hs, ht = cmid // 2, cout // 2

    def half_of(ref, size, which):
        return ref.at[pl.ds(pl.multiple_of(which * size, 8), size)]

    def tap_half(which):
        return tsum.at[pl.ds(low_tap, taps), pl.ds(pl.multiple_of(which * ht, 8), ht)]

    swap_s = remote(half_of(gsum, hs, 1 - n), nrs, ns.at[0], nr.at[0], w, 1 - n)
    swap_t = remote(tap_half(1 - n), nrt, ns.at[1], nr.at[1], w, 1 - n)
    swap_s.start()
    swap_t.start()
    swap_s.wait_recv()
    swap_t.wait_recv()
    mine_s = (gsum[pl.ds(pl.multiple_of(n * hs, 8), hs), :] + nrs[...]) * pscale
    mine_t = (tsum[pl.ds(low_tap, taps), pl.ds(pl.multiple_of(n * ht, 8), ht), :] + nrt[...]) * tscale
    main_s, last_s = fold_lanes(mine_s)
    main_t, last_t = fold_lanes(mine_t.reshape(taps * ht, cmid))
    flat = jnp.concatenate(main_s + main_t + last_s + last_t, axis=0)
    used = flat.shape[0]
    flat = jnp.concatenate([flat, jnp.zeros((W * rows - used, 128), F32)], axis=0)
    sbuf[...] = flat.astype(BF16)

    def chunk(i):
        return pl.ds(pl.multiple_of(i * rows, 16), rows)

    def rs_copy(dst):
        return remote(sbuf.at[chunk(dst)], rbuf.at[w], rs_s.at[dst], rs_r.at[w], dst, n)

    def start_rs(k, carry):
        rs_copy(lax.rem(w + k, W)).start()
        return carry

    lax.fori_loop(1, W, start_rs, 0)
    rbuf[w] = sbuf[chunk(w), :]

    def step(t, carry):
        a = apad[pl.ds(pl.multiple_of(2 * t * cmid, 16), taps * cmid), :]
        o = jnp.dot(wt_ref[...], a, preferred_element_type=F32) + tb
        out_ref[t] = o.astype(BF16)
        return carry

    lax.fori_loop(0, T, step, 0)

    def wait_rs(k, carry):
        src = lax.rem(w + W - k, W)
        remote(sbuf.at[chunk(src)], rbuf.at[src], rs_s.at[src], rs_r.at[src], src, n).wait_recv()
        return carry

    lax.fori_loop(1, W, wait_rs, 0)
    full[n, chunk(w), :] = jnp.sum(rbuf[...].astype(F32), axis=0).astype(BF16)

    def ag_copy(dst):
        return remote(full.at[n, chunk(w)], full.at[n, chunk(w)], ag_s.at[dst], ag_r.at[w], dst, n)

    def start_ag(k, carry):
        ag_copy(lax.rem(w + k, W)).start()
        return carry

    lax.fori_loop(1, W, start_ag, 0)

    def fw_copy(src):
        return remote(full.at[n, chunk(src)], full.at[n, chunk(src)], fw_s.at[src], fw_r.at[src], w, 1 - n)

    fw_copy(w).start()

    def relay(k, carry):
        src = lax.rem(w + W - k, W)
        remote(full.at[n, chunk(src)], full.at[n, chunk(src)], ag_s.at[src], ag_r.at[src], src, n).wait_recv()
        fw_copy(src).start()
        return carry

    lax.fori_loop(1, W, relay, 0)

    first = per * 2 * n

    def wait_gv(i, carry):
        @pl.when(first + i != me)
        def _():
            remote(gv.at[0], gvr_ref.at[pl.ds(i * tr, tr)], gv_s.at[0], gv_r.at[i], w, 1 - n).wait_recv()

        return carry

    lax.fori_loop(0, 2 * per, wait_gv, 0)

    def finish(k, carry):
        other = lax.rem(w + k, W)
        v_copy(other).wait_send()
        hand_on(other, lambda copy: copy.wait_send())
        rs_copy(other).wait_send()
        ag_copy(other).wait_send()
        gv_copy(other).wait_send()
        return carry

    lax.fori_loop(1, W, finish, 0)

    hand_on(w, lambda copy: copy.wait_send())

    def finish_fw(s, carry):
        remote(
            full.at[1 - n, chunk(s)], full.at[1 - n, chunk(s)], fw_s.at[s], fw_r.at[s], w, 1 - n
        ).wait_recv()
        fw_copy(s).wait_send()
        return carry

    lax.fori_loop(0, W, finish_fw, 0)
    down.wait_send()
    up.wait_send()
    swap_s.wait_send()
    swap_t.wait_send()

    @pl.when(goal == n)
    def _():
        mine.wait()

    @pl.when(goal != n)
    def _():
        gv_copy(w).wait_send()

    def spans(base, count, size):
        return [slice(base + i * size, base + (i + 1) * size) for i in range(count)]

    ns_blocks, nt_blocks = len(main_s), len(main_t)
    base_t = ns_blocks * hs
    base_ls = base_t + nt_blocks * taps * ht
    base_lt = base_ls + (last_s[0].shape[0] if last_s else 0)
    whole = full[n].astype(F32)
    gs_ref[...] = unfold_lanes(
        [whole[c] for c in spans(0, ns_blocks, hs)], whole[base_ls:base_lt], ws_ref.shape[1]
    )
    for h in range(2):
        whole = full[h].astype(F32)
        taps_h = unfold_lanes(
            [whole[c] for c in spans(base_t, nt_blocks, taps * ht)], whole[base_lt:used], cmid
        )
        gt_ref[:, h * ht : (h + 1) * ht, :] = taps_h.reshape(taps, ht, cmid)


def per_device(video, spatial_weight, spatial_bias, temporal_weight, temporal_bias, out_cotangent):
    W = lax.axis_size("wide")
    _, cin, R, cols = video.shape
    cmid = spatial_weight.shape[0]
    cout, taps, _ = temporal_weight.shape
    T = out_cotangent.shape[0]
    tr = out_cotangent.shape[2]
    F = W
    px = tr * cols
    half = taps // 2
    tscale = 1.0 / math.sqrt(T * R * cols)
    pscale = 1.0 / math.sqrt(F * R * cols)
    dma = pltpu.SemaphoreType.DMA
    vmem = pl.BlockSpec(memory_space=pltpu.VMEM)
    words = (cmid * 9 * cin + cout * taps * cmid) // 2
    rows = -(-words // (W * 128 * 16)) * 16

    v_rows = jnp.transpose(video[0], (1, 0, 2))
    g_rows = jnp.transpose(out_cotangent, (2, 0, 1, 3))
    ws = spatial_weight.reshape(cmid, 9 * cin)
    wt = temporal_weight.reshape(cout, taps * cmid)

    out, gv_rows, gs, gt = pl.pallas_call(
        functools.partial(block_kernel, W, tr, T, taps, rows, pscale, tscale),
        out_shape=(
            jax.ShapeDtypeStruct((T, cout, px), BF16),
            jax.ShapeDtypeStruct((R // 2, cin, cols), BF16),
            jax.ShapeDtypeStruct((cmid // 2, 9 * cin), F32),
            jax.ShapeDtypeStruct((taps, cout, cmid), F32),
        ),
        in_specs=[vmem] * 6,
        out_specs=(vmem,) * 4,
        scratch_shapes=[
            pltpu.VMEM((F, tr + 4, cin, cols), BF16),
            pltpu.VMEM((2, T, cout, cols), BF16),
            pltpu.VMEM((tr + 4, 3, cin, cols), BF16),
            pltpu.VMEM(((T + half + 1) * cout, (tr + 2) * cols), BF16),
            pltpu.VMEM(((F + 2 * half) * cmid, px), BF16),
            pltpu.VMEM((cmid, 9 * cin), F32),
            pltpu.VMEM((F + 2 * (T - 1), cout, cmid), F32),
            pltpu.VMEM((3, 3 * cin, cmid), BF16),
            pltpu.VMEM((2, cmid, (half + 1) * cout), BF16),
            pltpu.VMEM((F, tr, cin, cols), BF16),
            pltpu.VMEM((cmid // 2, 9 * cin), F32),
            pltpu.VMEM((taps, cout // 2, cmid), F32),
            pltpu.VMEM((W * rows, 128), BF16),
            pltpu.VMEM((W, rows, 128), BF16),
            pltpu.VMEM((2, W * rows, 128), BF16),
        ]
        + [dma((W,))] * 6
        + [dma((2,))] * 4
        + [dma((W,))] * 8
        + [dma],
        compiler_params=pltpu.CompilerParams(
            collective_id=0, has_side_effects=True, vmem_limit_bytes=VMEM_BYTES
        ),
        name="space_time_block",
    )(v_rows, g_rows, ws, spatial_bias[None], wt, temporal_bias[None])

    grad_spatial = gs.reshape(cmid // 2, 9, cin)
    grad_temporal = jnp.transpose(gt, (1, 0, 2))
    grad_video = jnp.transpose(gv_rows, (1, 0, 2))[None]
    output = out.reshape(T, cout, tr, cols)
    return (output, grad_video, grad_spatial, grad_temporal)


def solution(mesh):
    in_specs = (
        P(("grp", "wide"), None, None, None),
        P(),
        P(),
        P(),
        P(),
        P("grp", None, ("wide", "narrow"), None),
    )
    out_specs = (
        P("grp", None, ("wide", "narrow"), None),
        P(("grp", "wide"), None, "narrow", None),
        P(("grp", "narrow"), None, None),
        P("grp", None, None),
    )
    return jax.shard_map(
        per_device, mesh=mesh, in_specs=in_specs, out_specs=out_specs, check_vma=False
    )
```

```python
import functools
import math

import jax
import jax.numpy as jnp
from jax import lax
from jax.experimental import pallas as pl
from jax.experimental.pallas import tpu as pltpu
from jax.sharding import PartitionSpec as P

MESH = pl.DeviceIdType.MESH
BF16 = jnp.bfloat16
F32 = jnp.float32
VMEM_BYTES = 50 * 1024 * 1024


def greet_all(wide_count, between):
    me = lax.axis_index("wide") * 2 + lax.axis_index("narrow")
    total = 2 * wide_count
    barrier = pltpu.get_barrier_semaphore()

    def greet(k, carry):
        other = lax.rem(me + k, total)
        pl.semaphore_signal(
            barrier, inc=1, device_id={"wide": other // 2, "narrow": lax.rem(other, 2)}, device_id_type=MESH
        )
        return carry

    lax.fori_loop(1, total, greet, 0)
    between()
    pl.semaphore_wait(barrier, total - 1)


def remote(src, dst, send_sem, recv_sem, wide, narrow):
    return pltpu.make_async_remote_copy(
        src_ref=src,
        dst_ref=dst,
        send_sem=send_sem,
        recv_sem=recv_sem,
        device_id={"wide": wide, "narrow": narrow},
        device_id_type=MESH,
    )


def nt(a, b):
    return lax.dot_general(a, b, (((1,), (1,)), ((), ())), preferred_element_type=F32)


def fold_lanes(x):
    rows, lanes = x.shape
    blocks = lanes // 128
    parts = [x[:, 128 * b : 128 * (b + 1)] for b in range(blocks)]
    left = lanes - 128 * blocks
    if not left:
        return parts, []
    fold = 128 // left
    piece = rows // fold
    last = jnp.concatenate([x[piece * i : piece * (i + 1), 128 * blocks :] for i in range(fold)], axis=1)
    return parts, [last]


def unfold_lanes(parts, last, lanes):
    blocks = lanes // 128
    left = lanes - 128 * blocks
    if not left:
        return jnp.concatenate(parts, axis=1)
    fold = 128 // left
    end = jnp.concatenate([last[:, left * i : left * (i + 1)] for i in range(fold)], axis=0)
    return jnp.concatenate(parts + [end], axis=1)


def block_kernel(
    W, tr, T, taps, rows, pscale, tscale,
    v_ref, g_ref, ws_ref, sb_ref, wt_ref, tb_ref,
    out_ref, gvr_ref, gs_ref, gt_ref,
    slab, halo, stack, gpad, apad, gsum, tsum, wv, wtap, gv,
    nrs, nrt, sbuf, rbuf, full,
    v_s, v_r, vd_s, vd_r, vu_s, vu_r, h_s, h_r, ns, nr, rs_s, rs_r, ag_s, ag_r, fw_s, fw_r, gv_s, gv_r, lsem,
):
    F = W
    w = lax.axis_index("wide")
    n = lax.axis_index("narrow")
    me = w * 2 + n
    R, cin, cols = v_ref.shape
    cmid = ws_ref.shape[0]
    cout = wt_ref.shape[0]
    half = taps // 2
    lead = half // 2
    gp_rows = tr + 2
    px = tr * cols
    rows6 = tr + 4
    even_taps = half + 1
    per = W // 2
    goal = w // per
    spot = lax.rem(w, per) * 2 + n
    low_tap = 2 * (T - 1) - half

    def between():
        for i in range(3):
            wv[i] = ws_ref[:, 3 * cin * i : 3 * cin * (i + 1)].astype(F32).T.astype(BF16)

    greet_all(W, between)

    nxt = lax.rem(me + 1, 2 * W)
    prv = lax.rem(me + 2 * W - 1, 2 * W)
    down = remote(g_ref.at[tr - 1], halo.at[0], h_s.at[0], h_r.at[0], nxt // 2, lax.rem(nxt, 2))
    up = remote(g_ref.at[0], halo.at[1], h_s.at[1], h_r.at[1], prv // 2, lax.rem(prv, 2))
    down.start()
    up.start()

    def v_copy(dst):
        return remote(
            v_ref.at[pl.ds(2 * tr * dst + tr * n, tr)], slab.at[w, pl.ds(2, tr)], v_s.at[dst], v_r.at[w], dst, n
        )

    def v_arrival(src):
        return remote(v_ref.at[pl.ds(0, tr)], slab.at[src, pl.ds(2, tr)], v_s.at[src], v_r.at[src], src, n)

    def to_next(src):
        return remote(
            slab.at[src, pl.ds(tr, 2)], slab.at[src, pl.ds(0, 2)], vd_s.at[src], vd_r.at[src], nxt // 2, 1 - n
        )

    def to_prev(src):
        return remote(
            slab.at[src, pl.ds(2, 2)], slab.at[src, pl.ds(tr + 2, 2)], vu_s.at[src], vu_r.at[src], prv // 2, 1 - n
        )

    sends_down = me < 2 * W - 1
    sends_up = me > 0

    def hand_on(src, act):
        @pl.when(jnp.logical_and(sends_down, src != nxt // 2))
        def _():
            act(to_next(src))

        @pl.when(jnp.logical_and(sends_up, src != prv // 2))
        def _():
            act(to_prev(src))

    def await_halo(src):
        @pl.when(sends_up)
        def _():
            to_next(src).wait_recv()

        @pl.when(sends_down)
        def _():
            to_prev(src).wait_recv()

    def gv_copy(f):
        return remote(gv.at[f], gvr_ref.at[pl.ds(spot * tr, tr)], gv_s.at[f], gv_r.at[spot], f, goal)

    mine = pltpu.make_async_copy(gv.at[w], gvr_ref.at[pl.ds(spot * tr, tr)], lsem)

    def start(k, carry):
        v_copy(lax.rem(w + k, W)).start()
        return carry

    lax.fori_loop(1, W, start, 0)

    slab[w, 2 : 2 + tr] = v_ref[pl.ds(tr * me, tr)]
    hand_on(w, lambda copy: copy.start())
    edge = jnp.zeros((2, cin, cols), BF16)

    @pl.when(sends_up)
    def _():
        slab[w, 0:2] = v_ref[pl.ds(jnp.maximum(tr * me - 2, 0), 2)]

    @pl.when(sends_down)
    def _():
        slab[w, tr + 2 :] = v_ref[pl.ds(jnp.minimum(tr * me + tr, R - 2), 2)]

    @pl.when(jnp.logical_not(sends_up))
    def _():
        for f in range(F):
            slab[f, 0:2] = edge

    @pl.when(jnp.logical_not(sends_down))
    def _():
        for f in range(F):
            slab[f, tr + 2 :] = edge

    for parity in range(2):
        for m in range(even_taps):
            k = taps - 1 - parity - 2 * m
            spread = slice(m * cout, (m + 1) * cout)
            if k < 0:
                wtap[parity, :, spread] = jnp.zeros((cmid, cout), BF16)
            else:
                wtap[parity, :, spread] = wt_ref[:, k * cmid : (k + 1) * cmid].astype(F32).T.astype(BF16)
    gpad[0 : lead * cout, :] = jnp.zeros((lead * cout, gp_rows * cols), BF16)
    gpad[(lead + T) * cout :, :] = jnp.zeros(((lead + 1) * cout, gp_rows * cols), BF16)
    apad[0 : half * cmid, :] = jnp.zeros((half * cmid, px), BF16)
    apad[(half + F) * cmid :, :] = jnp.zeros((half * cmid, px), BF16)
    gsum[...] = jnp.zeros_like(gsum)
    tsum[...] = jnp.zeros_like(tsum)

    body = slice(lead * cout, (lead + T) * cout)
    for r in range(tr):
        gpad[body, (r + 1) * cols : (r + 2) * cols] = g_ref[r].reshape(T * cout, cols)
    down.wait_recv()
    up.wait_recv()
    above = halo[0].reshape(T * cout, cols)
    gpad[body, 0:cols] = jnp.where(me == 0, jnp.zeros_like(above), above)
    below = halo[1].reshape(T * cout, cols)
    gpad[body, (tr + 1) * cols :] = jnp.where(me == 2 * W - 1, jnp.zeros_like(below), below)

    sb = jnp.broadcast_to(sb_ref[...], (8, cmid)).T[:, 0:1]
    tb = jnp.broadcast_to(tb_ref[...], (8, cout)).T[:, 0:1]
    lane = lax.broadcasted_iota(jnp.int32, (rows6 * cin, cols), 1)
    lane_out = lax.broadcasted_iota(jnp.int32, (cin, cols), 1)

    def frame(f):
        x = slab[f].reshape(rows6 * cin, cols)
        xf = x.astype(F32)
        left = jnp.where(lane == 0, 0.0, pltpu.roll(xf, 1, 1)).astype(BF16)
        right = jnp.where(lane == cols - 1, 0.0, pltpu.roll(xf, cols - 1, 1)).astype(BF16)
        stack[:, 0] = left.reshape(rows6, cin, cols)
        stack[:, 1] = x.reshape(rows6, cin, cols)
        stack[:, 2] = right.reshape(rows6, cin, cols)
        big = jnp.concatenate(
            [stack[r : r + 3].reshape(9 * cin, cols) for r in range(gp_rows)], axis=1
        )
        pre = jnp.dot(ws_ref[...], big, preferred_element_type=F32) + sb
        s = 1.0 / (1.0 + jnp.exp(-pre))
        act = (pre[:, cols : cols + px] * s[:, cols : cols + px]).astype(BF16)
        apad[pl.ds(pl.multiple_of((f + half) * cmid, 16), cmid), :] = act
        odd = lax.rem(f, 2)
        g_start = pl.multiple_of((f // 2 + odd) * cout, 16)
        ga = jnp.dot(wtap[odd], gpad[pl.ds(g_start, even_taps * cout), :], preferred_element_type=F32)
        slope = s * (1.0 + pre * (1.0 - s))
        gp = (ga.astype(BF16).astype(F32) * slope).astype(BF16)
        z = jnp.dot(wv[2], gp[:, 0:px], preferred_element_type=F32)
        z += jnp.dot(wv[1], gp[:, cols : cols + px], preferred_element_type=F32)
        z += jnp.dot(wv[0], gp[:, 2 * cols : 2 * cols + px], preferred_element_type=F32)
        for r in range(tr):
            zr = z[:, r * cols : (r + 1) * cols]
            total = zr[cin : 2 * cin]
            total += jnp.where(lane_out == cols - 1, 0.0, pltpu.roll(zr[0:cin], cols - 1, 1))
            total += jnp.where(lane_out == 0, 0.0, pltpu.roll(zr[2 * cin :], 1, 1))
            gv[f, r] = total.astype(BF16)
        gsum[...] += nt(gp[:, cols : cols + px], big[:, cols : cols + px])
        pairs = nt(gpad[body, cols : cols + px], act)
        for t in range(T):
            at = f + 2 * (T - 1 - t)
            tsum[at] += pairs[t * cout : (t + 1) * cout]

    frame(w)

    @pl.when(goal == n)
    def _():
        mine.start()

    @pl.when(goal != n)
    def _():
        gv_copy(w).start()

    def take(k):
        src = lax.rem(w + 2 * W - k, W)
        v_arrival(src).wait_recv()
        hand_on(src, lambda copy: copy.start())

    for k in range(1, W):
        take(k)

    def each(k, carry):
        src = lax.rem(w + W - k, W)

        await_halo(src)
        frame(src)
        gv_copy(src).start()
        return carry

    lax.fori_loop(1, W, each, 0)

    hs, ht = cmid // 2, cout // 2

    def half_of(ref, size, which):
        return ref.at[pl.ds(pl.multiple_of(which * size, 8), size)]

    def tap_half(which):
        return tsum.at[pl.ds(low_tap, taps), pl.ds(pl.multiple_of(which * ht, 8), ht)]

    swap_s = remote(half_of(gsum, hs, 1 - n), nrs, ns.at[0], nr.at[0], w, 1 - n)
    swap_t = remote(tap_half(1 - n), nrt, ns.at[1], nr.at[1], w, 1 - n)
    swap_s.start()
    swap_t.start()
    swap_s.wait_recv()
    swap_t.wait_recv()
    mine_s = (gsum[pl.ds(pl.multiple_of(n * hs, 8), hs), :] + nrs[...]) * pscale
    mine_t = (tsum[pl.ds(low_tap, taps), pl.ds(pl.multiple_of(n * ht, 8), ht), :] + nrt[...]) * tscale
    main_s, last_s = fold_lanes(mine_s)
    main_t, last_t = fold_lanes(mine_t.reshape(taps * ht, cmid))
    flat = jnp.concatenate(main_s + main_t + last_s + last_t, axis=0)
    used = flat.shape[0]
    flat = jnp.concatenate([flat, jnp.zeros((W * rows - used, 128), F32)], axis=0)
    sbuf[...] = flat.astype(BF16)

    def chunk(i):
        return pl.ds(pl.multiple_of(i * rows, 16), rows)

    def rs_copy(dst):
        return remote(sbuf.at[chunk(dst)], rbuf.at[w], rs_s.at[dst], rs_r.at[w], dst, n)

    def start_rs(k, carry):
        rs_copy(lax.rem(w + k, W)).start()
        return carry

    lax.fori_loop(1, W, start_rs, 0)
    rbuf[w] = sbuf[chunk(w), :]

    def step(t, carry):
        a = apad[pl.ds(pl.multiple_of(2 * t * cmid, 16), taps * cmid), :]
        o = jnp.dot(wt_ref[...], a, preferred_element_type=F32) + tb
        out_ref[t] = o.astype(BF16)
        return carry

    lax.fori_loop(0, T, step, 0)

    def wait_rs(k, carry):
        src = lax.rem(w + W - k, W)
        remote(sbuf.at[chunk(src)], rbuf.at[src], rs_s.at[src], rs_r.at[src], src, n).wait_recv()
        return carry

    lax.fori_loop(1, W, wait_rs, 0)
    full[n, chunk(w), :] = jnp.sum(rbuf[...].astype(F32), axis=0).astype(BF16)

    def ag_copy(dst):
        return remote(full.at[n, chunk(w)], full.at[n, chunk(w)], ag_s.at[dst], ag_r.at[w], dst, n)

    def start_ag(k, carry):
        ag_copy(lax.rem(w + k, W)).start()
        return carry

    lax.fori_loop(1, W, start_ag, 0)

    def fw_copy(src):
        return remote(full.at[n, chunk(src)], full.at[n, chunk(src)], fw_s.at[src], fw_r.at[src], w, 1 - n)

    fw_copy(w).start()

    def relay(k, carry):
        src = lax.rem(w + W - k, W)
        remote(full.at[n, chunk(src)], full.at[n, chunk(src)], ag_s.at[src], ag_r.at[src], src, n).wait_recv()
        fw_copy(src).start()
        return carry

    lax.fori_loop(1, W, relay, 0)

    first = per * 2 * n

    def wait_gv(i, carry):
        @pl.when(first + i != me)
        def _():
            remote(gv.at[0], gvr_ref.at[pl.ds(i * tr, tr)], gv_s.at[0], gv_r.at[i], w, 1 - n).wait_recv()

        return carry

    lax.fori_loop(0, 2 * per, wait_gv, 0)

    def finish(k, carry):
        other = lax.rem(w + k, W)
        v_copy(other).wait_send()
        hand_on(other, lambda copy: copy.wait_send())
        rs_copy(other).wait_send()
        ag_copy(other).wait_send()
        gv_copy(other).wait_send()
        return carry

    lax.fori_loop(1, W, finish, 0)

    hand_on(w, lambda copy: copy.wait_send())

    def finish_fw(s, carry):
        remote(
            full.at[1 - n, chunk(s)], full.at[1 - n, chunk(s)], fw_s.at[s], fw_r.at[s], w, 1 - n
        ).wait_recv()
        fw_copy(s).wait_send()
        return carry

    lax.fori_loop(0, W, finish_fw, 0)
    down.wait_send()
    up.wait_send()
    swap_s.wait_send()
    swap_t.wait_send()

    @pl.when(goal == n)
    def _():
        mine.wait()

    @pl.when(goal != n)
    def _():
        gv_copy(w).wait_send()

    def spans(base, count, size):
        return [slice(base + i * size, base + (i + 1) * size) for i in range(count)]

    ns_blocks, nt_blocks = len(main_s), len(main_t)
    base_t = ns_blocks * hs
    base_ls = base_t + nt_blocks * taps * ht
    base_lt = base_ls + (last_s[0].shape[0] if last_s else 0)
    whole = full[n].astype(F32)
    gs_ref[...] = unfold_lanes(
        [whole[c] for c in spans(0, ns_blocks, hs)], whole[base_ls:base_lt], ws_ref.shape[1]
    )
    for h in range(2):
        whole = full[h].astype(F32)
        taps_h = unfold_lanes(
            [whole[c] for c in spans(base_t, nt_blocks, taps * ht)], whole[base_lt:used], cmid
        )
        gt_ref[:, h * ht : (h + 1) * ht, :] = taps_h.reshape(taps, ht, cmid)


def per_device(video, spatial_weight, spatial_bias, temporal_weight, temporal_bias, out_cotangent):
    W = lax.axis_size("wide")
    _, cin, R, cols = video.shape
    cmid = spatial_weight.shape[0]
    cout, taps, _ = temporal_weight.shape
    T = out_cotangent.shape[0]
    tr = out_cotangent.shape[2]
    F = W
    px = tr * cols
    half = taps // 2
    tscale = 1.0 / math.sqrt(T * R * cols)
    pscale = 1.0 / math.sqrt(F * R * cols)
    dma = pltpu.SemaphoreType.DMA
    vmem = pl.BlockSpec(memory_space=pltpu.VMEM)
    words = (cmid * 9 * cin + cout * taps * cmid) // 2
    rows = -(-words // (W * 128 * 16)) * 16

    v_rows = jnp.transpose(video[0], (1, 0, 2))
    g_rows = jnp.transpose(out_cotangent, (2, 0, 1, 3))
    ws = spatial_weight.reshape(cmid, 9 * cin)
    wt = temporal_weight.reshape(cout, taps * cmid)

    out, gv_rows, gs, gt = pl.pallas_call(
        functools.partial(block_kernel, W, tr, T, taps, rows, pscale, tscale),
        out_shape=(
            jax.ShapeDtypeStruct((T, cout, px), BF16),
            jax.ShapeDtypeStruct((R // 2, cin, cols), BF16),
            jax.ShapeDtypeStruct((cmid // 2, 9 * cin), F32),
            jax.ShapeDtypeStruct((taps, cout, cmid), F32),
        ),
        in_specs=[vmem] * 6,
        out_specs=(vmem,) * 4,
        scratch_shapes=[
            pltpu.VMEM((F, tr + 4, cin, cols), BF16),
            pltpu.VMEM((2, T, cout, cols), BF16),
            pltpu.VMEM((tr + 4, 3, cin, cols), BF16),
            pltpu.VMEM(((T + half + 1) * cout, (tr + 2) * cols), BF16),
            pltpu.VMEM(((F + 2 * half) * cmid, px), BF16),
            pltpu.VMEM((cmid, 9 * cin), F32),
            pltpu.VMEM((F + 2 * (T - 1), cout, cmid), F32),
            pltpu.VMEM((3, 3 * cin, cmid), BF16),
            pltpu.VMEM((2, cmid, (half + 1) * cout), BF16),
            pltpu.VMEM((F, tr, cin, cols), BF16),
            pltpu.VMEM((cmid // 2, 9 * cin), F32),
            pltpu.VMEM((taps, cout // 2, cmid), F32),
            pltpu.VMEM((W * rows, 128), BF16),
            pltpu.VMEM((W, rows, 128), BF16),
            pltpu.VMEM((2, W * rows, 128), BF16),
        ]
        + [dma((W,))] * 6
        + [dma((2,))] * 4
        + [dma((W,))] * 8
        + [dma],
        compiler_params=pltpu.CompilerParams(
            collective_id=0, has_side_effects=True, vmem_limit_bytes=VMEM_BYTES
        ),
        name="space_time_block",
    )(v_rows, g_rows, ws, spatial_bias[None], wt, temporal_bias[None])

    grad_spatial = gs.reshape(cmid // 2, 9, cin)
    grad_temporal = jnp.transpose(gt, (1, 0, 2))
    grad_video = jnp.transpose(gv_rows, (1, 0, 2))[None]
    output = out.reshape(T, cout, tr, cols)
    return (output, grad_video, grad_spatial, grad_temporal)


def solution(mesh):
    in_specs = (
        P(("grp", "wide"), None, None, None),
        P(),
        P(),
        P(),
        P(),
        P("grp", None, ("wide", "narrow"), None),
    )
    out_specs = (
        P("grp", None, ("wide", "narrow"), None),
        P(("grp", "wide"), None, "narrow", None),
        P(("grp", "narrow"), None, None),
        P("grp", None, None),
    )
    return jax.shard_map(
        per_device, mesh=mesh, in_specs=in_specs, out_specs=out_specs, check_vma=False
    )
```
